32 devices in a mesh: group: 2 (over y), cache: 4 (over z), tensor: 2 (over x), kvsplit: 2 (over core).
Axes of the slice: x: 2, y: 2, z: 4, core: 2. Of those that a mesh axis runs over, the one named last changes fastest.
Arguments:
- cache_kv: bfloat16 [32, 256, 4, 2, 128], P(('group', 'cache'), 'kvsplit', 'tensor'), parts along dimension 0, may hold values from -6 to 6
- passage_slot: int32 [32], P('group'), parts along dimension 0, may hold values from 0 to 15, as said below
- retrieval: int32 [8, 16], P(('group', 'cache')), parts along dimension 0, may hold values from 0 to 15, as said below
- recompute: int32 [8, 256], P(('group', 'cache')), parts along dimension 0, may hold values from 0 to 4095, as said below
- new_q: bfloat16 [8, 384, 32, 128], P(('group', 'cache'), None, 'tensor'), parts along dimension 0, may hold values from -10 to 10
- new_kv: bfloat16 [8, 384, 4, 2, 128], P(('group', 'cache'), 'kvsplit', 'tensor'), parts along dimension 0, may hold values from -6 to 6
Outputs:
- attended: bfloat16 [8, 384, 4096], P(('group', 'cache'), 'kvsplit', 'tensor'), parts along dimension 0
The draws below stay inside these ranges and needn't reach their ends.
There are 2 independent parts, one for each index of `group`. The reference program is written for one: setup_inputs(seed, part) draws one part's arguments, and reference() takes and returns one part's arrays. A program takes and returns all parts, laid end to end along the dimension named above; each array names one. Nothing has to cross between parts.
Inputs may be any that keep to these rules, and one draw needn't show every extreme that they name: `passage_slot`: each slot once. `retrieval`: among the 16 retrieved passages of the 1 request of one index of cache, at most 8 are stored on any one owner, and on every such index some owner stores exactly 8 of them. `recompute`: distinct and rising within a request.
All inputs are finite; a program needn't handle non-finite values.
Results may differ from the reference program's by a relative error of at most 0.0055.
Values may be sent and summed in bfloat16 or wider, within the bound.
A program may use at most 64 MiB of HBM per device.

```python
import jax
import jax.numpy as jnp
from jax import lax

HD = 128
QH = 32
KVH = 4
PLEN = 256
NPASS = 16
QLEN = 128
RC = 256
SLOTS = 4
REQS = 4
PASSAGES = 16
NEW = 384
CTX = 4096
ENTRIES = 16
CAP = 8
N_CACHE = 4


def corpus_layout(key):
    slot_order = jax.random.permutation(jax.random.fold_in(key, 101), PASSAGES).astype(jnp.int32)
    inverse = jnp.argsort(slot_order).astype(jnp.int32)

    def device_owners(device_key):
        busiest = jax.random.randint(jax.random.fold_in(device_key, 1), (), 0, N_CACHE)
        pooled = jnp.arange((N_CACHE - 1) * CAP, dtype=jnp.int32) // CAP
        pooled = pooled + (pooled >= busiest).astype(jnp.int32)
        shuffled = jax.random.permutation(jax.random.fold_in(device_key, 2), pooled)[:ENTRIES - CAP]
        owners = jnp.concatenate([jnp.full((CAP,), busiest, dtype=jnp.int32), shuffled])
        owners = jax.random.permutation(jax.random.fold_in(device_key, 3), owners)
        within = jax.random.randint(jax.random.fold_in(device_key, 4), (ENTRIES,), 0, SLOTS)
        return owners * SLOTS + within
    device_keys = jax.random.split(jax.random.fold_in(key, 102), N_CACHE)
    slot_ids = jax.vmap(device_owners)(device_keys)
    passage_ids = inverse[slot_ids].reshape(REQS, NPASS)
    return (slot_order, passage_ids.astype(jnp.int32))


def draw_passage_slot(key, part):
    slot_order, passage_ids = corpus_layout(key)
    return slot_order


def draw_retrieval(key, part):
    slot_order, passage_ids = corpus_layout(key)
    return passage_ids


def draw_recompute(key, part):
    key = jax.random.fold_in(key, 7)
    stride = CTX // RC
    offsets = jax.random.randint(key, (REQS, RC), 0, stride)
    return (jnp.arange(RC, dtype=jnp.int32)[None, :] * stride + offsets).astype(jnp.int32)


def draw_new_kv(key, part):
    key = jax.random.fold_in(key, 11)
    values = jnp.clip(jax.random.normal(key, (REQS, NEW, KVH, 2, HD), jnp.float32), -6.0, 6.0)
    return values.astype(jnp.bfloat16)


def draw_new_q(key, part):
    key = jax.random.fold_in(key, 13)
    queries = jnp.clip(jax.random.normal(key, (REQS, NEW, QH, HD), jnp.float32), -5.0, 5.0)
    return queries.astype(jnp.bfloat16)


def levels(rng, dims, shards, least, largest):
    gain, own = 1.0, jax.random.fold_in(rng, 6)
    for dim, shards_of in shards:
        heights = jnp.exp(jax.random.uniform(jax.random.fold_in(own, dim), (shards_of,), jnp.float32, least / len(shards), largest / len(shards)))
        gain = gain * jnp.repeat(heights, dims[dim] // shards_of).reshape([-1 if axis == dim else 1 for axis in range(len(dims))])
    return gain


def normal_values(own_key, extent, deviation, limit, cuts=(), kind=jnp.bfloat16):
    factor_of = levels(own_key, extent, cuts, -0.22, 0.18) if cuts else 1.0
    drawn = jax.random.normal(own_key, extent, jnp.float32) * deviation * factor_of
    return jnp.minimum(jnp.maximum(drawn, -limit), limit).astype(kind)


def setup_inputs(seed: int = 0, part: int = 0) -> dict:
    streams_of = jax.random.split(jax.random.key(seed), 7)
    part_splits = jax.random.split(jax.random.fold_in(streams_of[6], part), 7)
    cache_kv = normal_values(part_splits[0], (PASSAGES, PLEN, KVH, 2, HD), 1.0, 6.0, ((0, 4), (1, 2), (2, 2)))
    passage_slot = draw_passage_slot(jax.random.fold_in(jax.random.fold_in(streams_of[6], part), 71), part)
    retrieval = draw_retrieval(jax.random.fold_in(jax.random.fold_in(streams_of[6], part), 71), part)
    recompute = draw_recompute(jax.random.fold_in(jax.random.fold_in(streams_of[6], part), 71), part)
    new_q = draw_new_q(jax.random.fold_in(jax.random.fold_in(streams_of[6], part), 71), part)
    new_kv = draw_new_kv(jax.random.fold_in(jax.random.fold_in(streams_of[6], part), 71), part)
    return dict(cache_kv=cache_kv, passage_slot=passage_slot, retrieval=retrieval, recompute=recompute, new_q=new_q, new_kv=new_kv)


def attend_request(cache_kv, slot_row, chosen, queries, fresh):
    context = cache_kv[slot_row].reshape(CTX, KVH, 2, HD)
    all_keys = jnp.concatenate([context, fresh], axis=0)
    chosen_pos = chosen.astype(jnp.int32)
    question = CTX + jnp.arange(QLEN, dtype=jnp.int32)
    query_pos = jnp.concatenate([chosen_pos, question])
    context_pos = jnp.arange(CTX, dtype=jnp.int32)
    key_pos = jnp.concatenate([context_pos, query_pos])
    replaced = jnp.any(context_pos[:, None] == chosen_pos[None, :], axis=1)
    key_live = jnp.concatenate([jnp.logical_not(replaced), jnp.ones((NEW,), dtype=bool)])
    allowed = key_live[None, :] & (key_pos[None, :] <= query_pos[:, None])
    grouped = queries.astype(jnp.float32).reshape(NEW, KVH, QH // KVH, HD)
    key_part = all_keys[:, :, 0, :].astype(jnp.float32)
    value_part = all_keys[:, :, 1, :].astype(jnp.float32)
    scores = jnp.einsum("nkgd,mkd->kgnm", grouped, key_part) * (HD ** -0.5)
    masked = jnp.where(allowed, scores, -1e30)
    row_max = jnp.max(masked, axis=-1, keepdims=True)
    weights = jnp.where(allowed, jnp.exp(masked - row_max), 0.0)
    totals = jnp.sum(weights, axis=-1)
    rounded = lax.optimization_barrier(weights.astype(jnp.bfloat16))
    weighted = jnp.einsum("kgnm,mkd->nkgd", rounded.astype(jnp.float32), value_part)
    result = weighted / jnp.transpose(totals, (2, 0, 1))[..., None]
    return result.reshape(NEW, QH * HD).astype(jnp.bfloat16)


def reference(cache_kv, passage_slot, retrieval, recompute, new_q, new_kv):
    slot_ids = passage_slot[retrieval]

    def one_request(packed):
        slot_row, chosen, queries, fresh = packed
        return attend_request(cache_kv, slot_row, chosen, queries, fresh)

    return lax.map(one_request, (slot_ids, recompute, new_q, new_kv))
```

```python
import functools
import math

import jax
import jax.numpy as jnp
from jax import lax
from jax.experimental import pallas as pl
from jax.experimental.pallas import tpu as pltpu
from jax.sharding import PartitionSpec as P

MASKED = -1e30


def attend(q_ref, keys, values, bias, acc_ref, max_ref, first, score_scale, pair):
    heads, rows, head_dim = q_ref.shape
    kv_local = keys.shape[0]
    pairs = heads // pair

    def turn(i, carry):
        at = pl.ds(i * pair, pair)
        kv = i // (pairs // kv_local)
        query = q_ref[at].reshape(pair * rows, head_dim)
        scores = lax.dot_general(
            query, keys[kv], (((1,), (1,)), ((), ())), preferred_element_type=jnp.float32
        )
        scores = scores.reshape(pair, rows, -1) * score_scale + bias[...][None]
        block_max = jnp.max(scores, axis=2, keepdims=True)
        if first:
            row_max = jnp.broadcast_to(block_max, (pair, rows, head_dim))
        else:
            former = max_ref[at]
            row_max = jnp.maximum(former, block_max)
        weights = jnp.exp2(scores - row_max[:, :, :1]).astype(jnp.bfloat16)
        part = jnp.dot(
            weights.reshape(pair * rows, -1), values[kv], preferred_element_type=jnp.float32
        ).reshape(pair, rows, 2 * head_dim)
        if first:
            acc_ref[at] = part
        else:
            shrink = jnp.exp2(former - row_max)
            acc_ref[at] = acc_ref[at] * jnp.concatenate([shrink, shrink], axis=2) + part
        max_ref[at] = row_max
        return carry

    lax.fori_loop(0, pairs, turn, 0, unroll=2)


def kernel(score_scale, pair, q_ref, fresh_ref, corpus_ref, fresh_bias, bias_ref, out_ref,
           acc_ref, max_ref, key_ref, value_ref, fresh_value):
    step = pl.program_id(0)
    heads, rows, head_dim = q_ref.shape
    kv_local = fresh_ref.shape[0]
    half = corpus_ref.shape[4]

    @pl.when(step == 0)
    def _():
        value_ref[...] = jnp.ones_like(value_ref)
        fresh_value[...] = jnp.ones_like(fresh_value)
        fresh_value[:, :, :head_dim] = fresh_ref[:, 1]
        attend(q_ref, fresh_ref.at[:, 0], fresh_value, fresh_bias, acc_ref, max_ref, True,
               score_scale, pair)

    for part in range(2):
        at = pl.ds(part * half, half)
        key_ref[:, at, :] = corpus_ref[0, part, :, 0]
        value_ref[:, at, :head_dim] = corpus_ref[0, part, :, 1]
    attend(q_ref, key_ref, value_ref, bias_ref.at[0], acc_ref, max_ref, False, score_scale, pair)

    @pl.when(step == pl.num_programs(0) - 1)
    def _():
        for head in range(heads):
            total = acc_ref[head]
            out_ref[:, head * head_dim:(head + 1) * head_dim] = (
                total[:, :head_dim] / total[:, head_dim:]
            ).astype(out_ref.dtype)


def on_device(cache_kv, passage_slot, retrieval, recompute, new_q, new_kv):
    slots, half_len, kv_local, _, head_dim = cache_kv.shape
    npass = retrieval.shape[1]
    new_rows, heads = new_q.shape[1:3]
    rc_rows = recompute.shape[1]
    owners = lax.axis_size("cache")
    holders = lax.axis_size("kvsplit")
    half_index = lax.axis_index("kvsplit")
    plen = half_len * holders
    ctx = npass * plen
    rows = new_rows // holders

    own = cache_kv.transpose(2, 3, 0, 1, 4).reshape(kv_local, 2, slots * half_len, head_dim)
    corpus = lax.all_gather(own, "cache", axis=0)
    corpus = lax.all_gather(corpus, "kvsplit", axis=1)
    fresh = lax.all_gather(new_kv[0].transpose(1, 2, 0, 3), "kvsplit", axis=2, tiled=True)

    passages = jnp.arange(passage_slot.shape[0], dtype=jnp.int32)
    chosen = jnp.sum(
        jnp.where(retrieval[0][:, None] == passages[None, :], passage_slot[None, :], 0), axis=1
    )
    question = ctx + jnp.arange(new_rows - rc_rows, dtype=jnp.int32)
    row_pos = jnp.concatenate([recompute[0], question])
    row_pos = lax.dynamic_slice_in_dim(row_pos, half_index * rows, rows, 0)
    row_pass, row_off = row_pos // plen, row_pos % plen
    context = jnp.arange(ctx, dtype=jnp.int32)
    live = jnp.logical_not(jnp.any(context[:, None] == recompute[0][None, :], axis=1))
    live = live.reshape(npass, holders, half_len).astype(jnp.bfloat16)
    entry = jnp.arange(npass, dtype=jnp.int32)
    before = (entry[None, :] < row_pass[:, None]).astype(jnp.bfloat16)
    within = (entry[None, :] == row_pass[:, None])
    row_slot = jnp.sum(jnp.where(within, chosen[None, :] + 1, 0), axis=1) - 1
    slot = jnp.arange(owners * slots, dtype=jnp.int32).reshape(owners, slots)
    held = (chosen[:, None, None] == slot[None]).astype(jnp.bfloat16)
    stored = held[:, :, None, :, None] * live[:, None, :, None, :]
    keys = holders * slots * half_len
    count = jnp.einsum("rj,jok->ork", before, stored.reshape(npass, owners, keys),
                       preferred_element_type=jnp.float32)
    edge = jnp.einsum("rj,jht->rht", within.astype(jnp.bfloat16), live,
                      preferred_element_type=jnp.float32)
    token = jnp.arange(plen, dtype=jnp.int32).reshape(holders, half_len)
    edge = jnp.where(token[None] <= row_off[:, None, None], edge, 0.0)
    mine = row_slot[None, :, None] == slot[:, None, :]
    extra = jnp.where(mine[:, :, None, :, None], edge[None, :, :, None, :], 0.0)
    count = count + extra.reshape(owners, rows, keys)
    bias = jnp.where(count > 0.5, jnp.log2(jnp.maximum(count, 1.0)), MASKED)
    new_index = jnp.arange(new_rows, dtype=jnp.int32)
    row_index = half_index * rows + jnp.arange(rows, dtype=jnp.int32)
    fresh_bias = jnp.where(new_index[None, :] <= row_index[:, None], 0.0, MASKED)

    queries = lax.dynamic_slice_in_dim(new_q[0], half_index * rows, rows, 0).transpose(1, 0, 2)
    score_scale = head_dim ** (-0.5) * math.log2(math.e)
    whole = lambda *shape: pl.BlockSpec(shape, lambda i: (0,) * len(shape))
    result = pl.pallas_call(
        functools.partial(kernel, score_scale, 2),
        grid=(owners,),
        out_shape=jax.ShapeDtypeStruct((rows, heads * head_dim), jnp.bfloat16),
        in_specs=[
            whole(heads, rows, head_dim),
            whole(kv_local, 2, new_rows, head_dim),
            pl.BlockSpec((1, holders, kv_local, 2, slots * half_len, head_dim),
                         lambda i: (i, 0, 0, 0, 0, 0)),
            whole(rows, new_rows),
            pl.BlockSpec((1, rows, keys), lambda i: (i, 0, 0)),
        ],
        out_specs=whole(rows, heads * head_dim),
        scratch_shapes=[
            pltpu.VMEM((heads, rows, 2 * head_dim), jnp.float32),
            pltpu.VMEM((heads, rows, head_dim), jnp.float32),
            pltpu.VMEM((kv_local, keys, head_dim), jnp.bfloat16),
            pltpu.VMEM((kv_local, keys, 2 * head_dim), jnp.bfloat16),
            pltpu.VMEM((kv_local, new_rows, 2 * head_dim), jnp.bfloat16),
        ],
        compiler_params=pltpu.CompilerParams(vmem_limit_bytes=48 * 1024 * 1024),
    )(queries, fresh, corpus, fresh_bias, bias)
    return result[None]


def solution(mesh):
    in_specs = (
        P(("group", "cache"), "kvsplit", "tensor", None, None),
        P("group"),
        P(("group", "cache"), None),
        P(("group", "cache"), None),
        P(("group", "cache"), None, "tensor", None),
        P(("group", "cache"), "kvsplit", "tensor", None, None),
    )
    out_specs = P(("group", "cache"), "kvsplit", "tensor")
    return jax.shard_map(
        on_device, mesh=mesh, in_specs=in_specs, out_specs=out_specs, check_vma=False
    )
```

```python
import functools
import math

import jax
import jax.numpy as jnp
from jax import lax
from jax.experimental import pallas as pl
from jax.experimental.pallas import tpu as pltpu
from jax.sharding import PartitionSpec as P

MASKED = -1e30


MESH = pl.DeviceIdType.MESH


def attend(q_ref, kv, keys, value_ref, bias_ref, acc_ref, max_ref, first, score_scale, pair):
    heads, rows, head_dim = q_ref.shape
    group = heads // keys[1]
    pairs = group // pair

    def turn(i, carry):
        at = pl.ds(kv * group + i * pair, pair)
        query = q_ref[at].reshape(pair * rows, head_dim)
        scores = lax.dot_general(
            query, keys[0](), (((1,), (1,)), ((), ())), preferred_element_type=jnp.float32
        )
        scores = scores.reshape(pair, rows, -1) * score_scale + bias_ref[...][None]
        block_max = jnp.max(scores, axis=2, keepdims=True)
        if first:
            row_max = jnp.broadcast_to(block_max, (pair, rows, head_dim))
        else:
            former = max_ref[at]
            row_max = jnp.maximum(former, block_max)
        weights = jnp.exp2(scores - row_max[:, :, :1]).astype(jnp.bfloat16)
        part = jnp.dot(
            weights.reshape(pair * rows, -1), value_ref[...], preferred_element_type=jnp.float32
        ).reshape(pair, rows, 2 * head_dim)
        if first:
            acc_ref[at] = part
        else:
            shrink = jnp.exp2(former - row_max)
            acc_ref[at] = acc_ref[at] * jnp.concatenate([shrink, shrink], axis=2) + part
        max_ref[at] = row_max
        return carry

    lax.fori_loop(0, pairs, turn, 0, unroll=2)


def kernel(score_scale, pair, owners, q_ref, fresh_ref, own_ref, stored_ref, live_ref, before_ref,
           within_ref, slot_ref, offset_ref, out_ref,
           acc_ref, max_ref, value_ref, new_value_ref, bias_ref, new_bias_ref, edge_ref,
           corpus_ref, new_ref, line_send, line_recv, side_send, side_recv, new_send, new_recv):
    heads, rows, head_dim = q_ref.shape
    kv_local, _, half, _ = own_ref.shape
    new_half = fresh_ref.shape[2]
    plen = live_ref.shape[1]
    half_len = plen // 2
    slots = half // half_len
    z = lax.axis_index("cache")
    mine = lax.axis_index("kvsplit")
    other = 1 - mine
    has_left, has_right = z > 0, z < owners - 1

    barrier = pltpu.get_barrier_semaphore()
    pl.semaphore_signal(barrier, inc=1, device_id={"kvsplit": other}, device_id_type=MESH)

    @pl.when(has_left)
    def _():
        pl.semaphore_signal(barrier, inc=1, device_id={"cache": z - 1}, device_id_type=MESH)

    @pl.when(has_right)
    def _():
        pl.semaphore_signal(barrier, inc=1, device_id={"cache": z + 1}, device_id_type=MESH)

    peers = 1 + jnp.minimum(z, 1) + jnp.minimum(owners - 1 - z, 1)
    pl.semaphore_wait(barrier, peers)

    def line_copy(block, owner, kv, way):
        return pltpu.make_async_remote_copy(
            src_ref=block, dst_ref=corpus_ref.at[owner, mine, kv],
            send_sem=line_send.at[way, owner, kv], recv_sem=line_recv.at[owner, kv],
            device_id={"cache": z + 1 if way else z - 1}, device_id_type=MESH)

    def side_copy(block, owner, kv):
        return pltpu.make_async_remote_copy(
            src_ref=block, dst_ref=corpus_ref.at[owner, mine, kv],
            send_sem=side_send.at[owner, kv], recv_sem=side_recv.at[owner, kv],
            device_id={"kvsplit": other}, device_id_type=MESH)

    new_copy = pltpu.make_async_remote_copy(
        src_ref=fresh_ref, dst_ref=new_ref.at[mine], send_sem=new_send, recv_sem=new_recv,
        device_id={"kvsplit": other}, device_id_type=MESH)

    for kv in range(kv_local):
        @pl.when(has_left)
        def _():
            line_copy(own_ref.at[kv], z, kv, 0).start()

        @pl.when(has_right)
        def _():
            line_copy(own_ref.at[kv], z, kv, 1).start()

    new_copy.start()
    for kv in range(kv_local):
        side_copy(own_ref.at[kv], z, kv).start()

    near = jnp.minimum(z, owners - 1 - z)

    def source(k):
        both = k < 2 * near
        far = jnp.where(both, k // 2 + 1, k - near + 1)
        left = jnp.where(both, k % 2, jnp.where(z > owners - 1 - z, 0, 1)) == 0
        return jnp.where(left, z - far, z + far), left

    def arrive(k, kv):
        owner, left = source(k)
        block = corpus_ref.at[owner, mine, kv]
        side = side_copy(block, owner, kv)
        line_copy(block, owner, kv, 1).wait_recv()

        @pl.when(jnp.logical_and(left, has_right))
        def _():
            line_copy(block, owner, kv, 1).start()

        @pl.when(jnp.logical_and(jnp.logical_not(left), has_left))
        def _():
            line_copy(block, owner, kv, 0).start()

        side.start()

    def compute(owner, kv):
        side_copy(corpus_ref.at[owner, mine, kv], owner, kv).wait_recv()
        if kv == 0:
            count = jnp.dot(before_ref[...], stored_ref[owner],
                            preferred_element_type=jnp.float32)
            for h in range(2):
                edge = edge_ref[:, h * half_len:(h + 1) * half_len]
                for s in range(slots):
                    at = slice((h * slots + s) * half_len, (h * slots + s + 1) * half_len)
                    total = count[:, at] + jnp.where(
                        slot_ref[...] == owner * slots + s, edge, 0.0)
                    bias_ref[:, at] = jnp.where(
                        total > 0.5, jnp.log2(jnp.maximum(total, 1.0)), MASKED)
        for h in range(2):
            value_ref[h * half:(h + 1) * half, :head_dim] = corpus_ref[owner, h, kv, 1]
        keys = lambda: corpus_ref[owner, :, kv, 0].reshape(2 * half, head_dim)
        attend(q_ref, kv, (keys, kv_local), value_ref, bias_ref, acc_ref, max_ref, False,
               score_scale, pair)

    corpus_ref[z, mine] = own_ref[...]
    new_ref[mine] = fresh_ref[...]
    value_ref[:, head_dim:] = jnp.ones((2 * half, head_dim), jnp.bfloat16)
    new_value_ref[:, head_dim:] = jnp.ones((2 * new_half, head_dim), jnp.bfloat16)
    token = lax.broadcasted_iota(jnp.int32, (rows, plen), 1)
    edge_ref[...] = jnp.where(
        token <= offset_ref[...],
        jnp.dot(within_ref[...], live_ref[...], preferred_element_type=jnp.float32), 0.0)
    row = lax.broadcasted_iota(jnp.int32, (rows, 2 * new_half), 0) + mine * rows
    column = lax.broadcasted_iota(jnp.int32, (rows, 2 * new_half), 1)
    new_bias_ref[...] = jnp.where(column <= row, 0.0, MASKED)

    new_copy.wait_recv()
    for kv in range(kv_local):
        for h in range(2):
            new_value_ref[h * new_half:(h + 1) * new_half, :head_dim] = new_ref[h, kv, 1]
        keys = lambda: new_ref[:, kv, 0].reshape(2 * new_half, head_dim)
        attend(q_ref, kv, (keys, kv_local), new_value_ref, new_bias_ref, acc_ref, max_ref, True,
               score_scale, pair)

    for kv in range(kv_local - 1):
        compute(z, kv)

    def turn(k, carry):
        for kv in range(kv_local):
            arrive(k, kv)
            if kv == 0:
                compute(jnp.where(k == 0, z, source(jnp.maximum(k - 1, 0))[0]), kv_local - 1)
            else:
                compute(source(k)[0], kv - 1)
        return carry

    lax.fori_loop(0, owners - 1, turn, 0)
    compute(source(owners - 2)[0], kv_local - 1)

    for head in range(heads):
        total = acc_ref[head]
        out_ref[:, head * head_dim:(head + 1) * head_dim] = (
            total[:, :head_dim] / total[:, head_dim:]
        ).astype(out_ref.dtype)

    for kv in range(kv_local):
        @pl.when(has_left)
        def _():
            line_copy(own_ref.at[kv], z, kv, 0).wait_send()

        @pl.when(has_right)
        def _():
            line_copy(own_ref.at[kv], z, kv, 1).wait_send()

        side_copy(own_ref.at[kv], z, kv).wait_send()
    new_copy.wait_send()

    def sent(k, carry):
        owner, left = source(k)
        for kv in range(kv_local):
            block = corpus_ref.at[owner, mine, kv]

            @pl.when(jnp.logical_and(left, has_right))
            def _():
                line_copy(block, owner, kv, 1).wait_send()

            @pl.when(jnp.logical_and(jnp.logical_not(left), has_left))
            def _():
                line_copy(block, owner, kv, 0).wait_send()

            side_copy(block, owner, kv).wait_send()
        return carry

    lax.fori_loop(0, owners - 1, sent, 0)


def on_device(cache_kv, passage_slot, retrieval, recompute, new_q, new_kv):
    slots, half_len, kv_local, _, head_dim = cache_kv.shape
    npass = retrieval.shape[1]
    new_rows, heads = new_q.shape[1:3]
    rc_rows = recompute.shape[1]
    owners = lax.axis_size("cache")
    holders = lax.axis_size("kvsplit")
    half_index = lax.axis_index("kvsplit")
    plen = half_len * holders
    ctx = npass * plen
    rows = new_rows // holders

    own = cache_kv.transpose(2, 3, 0, 1, 4).reshape(kv_local, 2, slots * half_len, head_dim)
    fresh = new_kv[0].transpose(1, 2, 0, 3)

    passages = jnp.arange(passage_slot.shape[0], dtype=jnp.int32)
    chosen = jnp.sum(
        jnp.where(retrieval[0][:, None] == passages[None, :], passage_slot[None, :], 0), axis=1
    )
    question = ctx + jnp.arange(new_rows - rc_rows, dtype=jnp.int32)
    row_pos = jnp.concatenate([recompute[0], question])
    row_pos = lax.dynamic_slice_in_dim(row_pos, half_index * rows, rows, 0)
    row_pass, row_off = row_pos // plen, row_pos % plen
    context = jnp.arange(ctx, dtype=jnp.int32)
    live = jnp.logical_not(jnp.any(context[:, None] == recompute[0][None, :], axis=1))
    live = live.reshape(npass, holders, half_len).astype(jnp.bfloat16)
    entry = jnp.arange(npass, dtype=jnp.int32)
    before = (entry[None, :] < row_pass[:, None]).astype(jnp.bfloat16)
    within = (entry[None, :] == row_pass[:, None])
    row_slot = jnp.sum(jnp.where(within, chosen[None, :] + 1, 0), axis=1) - 1
    slot = jnp.arange(owners * slots, dtype=jnp.int32).reshape(owners, slots)
    keys = holders * slots * half_len
    held = (chosen[None, :, None] == slot[:, None, :]).astype(jnp.bfloat16)
    stored = held[:, :, None, :, None] * live[None, :, :, None, :]
    stored = stored.reshape(owners, npass, keys)

    queries = lax.dynamic_slice_in_dim(new_q[0], half_index * rows, rows, 0).transpose(1, 0, 2)
    score_scale = head_dim ** (-0.5) * math.log2(math.e)
    dma = pltpu.SemaphoreType.DMA
    result = pl.pallas_call(
        functools.partial(kernel, score_scale, 2, owners),
        out_shape=jax.ShapeDtypeStruct((rows, heads * head_dim), jnp.bfloat16),
        in_specs=[pl.BlockSpec(memory_space=pltpu.VMEM)] * 9,
        out_specs=pl.BlockSpec(memory_space=pltpu.VMEM),
        scratch_shapes=[
            pltpu.VMEM((heads, rows, 2 * head_dim), jnp.float32),
            pltpu.VMEM((heads, rows, head_dim), jnp.float32),
            pltpu.VMEM((keys, 2 * head_dim), jnp.bfloat16),
            pltpu.VMEM((new_rows, 2 * head_dim), jnp.bfloat16),
            pltpu.VMEM((rows, keys), jnp.float32),
            pltpu.VMEM((rows, new_rows), jnp.float32),
            pltpu.VMEM((rows, plen), jnp.float32),
            pltpu.VMEM((owners, holders) + own.shape, jnp.bfloat16),
            pltpu.VMEM((holders,) + fresh.shape, jnp.bfloat16),
            dma((2, owners, kv_local)),
            dma((owners, kv_local)),
            dma((owners, kv_local)),
            dma((owners, kv_local)),
            dma(()),
            dma(()),
        ],
        compiler_params=pltpu.CompilerParams(
            vmem_limit_bytes=56 * 1024 * 1024, collective_id=0, has_side_effects=True),
    )(queries, fresh, own, stored, live.reshape(npass, plen), before,
      within.astype(jnp.bfloat16), row_slot[:, None], row_off[:, None])
    return result[None]


def solution(mesh):
    in_specs = (
        P(("group", "cache"), "kvsplit", "tensor", None, None),
        P("group"),
        P(("group", "cache"), None),
        P(("group", "cache"), None),
        P(("group", "cache"), None, "tensor", None),
        P(("group", "cache"), "kvsplit", "tensor", None, None),
    )
    out_specs = P(("group", "cache"), "kvsplit", "tensor")
    return jax.shard_map(
        on_device, mesh=mesh, in_specs=in_specs, out_specs=out_specs, check_vma=False
    )
```

```python
import functools
import math

import jax
import jax.numpy as jnp
from jax import lax
from jax.experimental import pallas as pl
from jax.experimental.pallas import tpu as pltpu
from jax.sharding import PartitionSpec as P

MASKED = -1e30


MESH = pl.DeviceIdType.MESH


def attend(q_ref, kv, keys, value_ref, bias_ref, acc_ref, max_ref, first, score_scale, pair):
    heads, rows, head_dim = q_ref.shape
    group = heads // keys[1]
    pairs = group // pair

    for i in range(pairs):
        at = slice(kv * group + i * pair, kv * group + (i + 1) * pair)
        query = q_ref[at].reshape(pair * rows, head_dim)
        scores = lax.dot_general(
            query, keys[0](), (((1,), (1,)), ((), ())), preferred_element_type=jnp.float32
        )
        scores = scores.reshape(pair, rows, -1) * score_scale + bias_ref[...][None]
        block_max = jnp.max(scores, axis=2, keepdims=True)
        if first:
            row_max = jnp.broadcast_to(block_max, (pair, rows, head_dim))
        else:
            former = max_ref[at]
            row_max = jnp.maximum(former, block_max)
        weights = jnp.exp2(scores - row_max[:, :, :1]).astype(jnp.bfloat16)
        part = jnp.dot(
            weights.reshape(pair * rows, -1), value_ref[...], preferred_element_type=jnp.float32
        ).reshape(pair, rows, 2 * head_dim)
        if first:
            acc_ref[at] = part
        else:
            shrink = jnp.exp2(former - row_max)
            acc_ref[at] = acc_ref[at] * jnp.concatenate([shrink, shrink], axis=2) + part
        max_ref[at] = row_max


def kernel(score_scale, pair, owners, q_ref, fresh_ref, own_ref, place_ref, chosen_ref, again_ref,
           out_ref,
           acc_ref, max_ref, value_ref, new_value_ref, bias_ref, new_bias_ref, edge_ref,
           live_ref, before_ref, slot_ref, entry_ref, corpus_ref, new_ref, line_send, line_recv, side_send, side_recv, new_send, new_recv):
    heads, rows, head_dim = q_ref.shape
    kv_local, _, half, _ = own_ref.shape
    new_half = fresh_ref.shape[2]
    plen = live_ref.shape[1]
    half_len = plen // 2
    slots = half // half_len
    z = lax.axis_index("cache")
    mine = lax.axis_index("kvsplit")
    other = 1 - mine
    has_left, has_right = z > 0, z < owners - 1

    barrier = pltpu.get_barrier_semaphore()
    pl.semaphore_signal(barrier, inc=1, device_id={"kvsplit": other}, device_id_type=MESH)

    @pl.when(has_left)
    def _():
        pl.semaphore_signal(barrier, inc=1, device_id={"cache": z - 1}, device_id_type=MESH)

    @pl.when(has_right)
    def _():
        pl.semaphore_signal(barrier, inc=1, device_id={"cache": z + 1}, device_id_type=MESH)

    peers = 1 + jnp.minimum(z, 1) + jnp.minimum(owners - 1 - z, 1)
    pl.semaphore_wait(barrier, peers)

    def line_copy(block, owner, kv, way):
        return pltpu.make_async_remote_copy(
            src_ref=block, dst_ref=corpus_ref.at[owner, mine, kv],
            send_sem=line_send.at[way, owner, kv], recv_sem=line_recv.at[owner, kv],
            device_id={"cache": z + 1 if way else z - 1}, device_id_type=MESH)

    def side_copy(block, owner, kv):
        return pltpu.make_async_remote_copy(
            src_ref=block, dst_ref=corpus_ref.at[owner, mine, kv],
            send_sem=side_send.at[owner, kv], recv_sem=side_recv.at[owner, kv],
            device_id={"kvsplit": other}, device_id_type=MESH)

    new_copy = pltpu.make_async_remote_copy(
        src_ref=fresh_ref, dst_ref=new_ref.at[mine], send_sem=new_send, recv_sem=new_recv,
        device_id={"kvsplit": other}, device_id_type=MESH)

    for kv in range(kv_local):
        @pl.when(has_left)
        def _():
            line_copy(own_ref.at[kv], z, kv, 0).start()

        @pl.when(has_right)
        def _():
            line_copy(own_ref.at[kv], z, kv, 1).start()

    new_copy.start()
    for kv in range(kv_local):
        side_copy(own_ref.at[kv], z, kv).start()

    near = jnp.minimum(z, owners - 1 - z)

    def source(k):
        both = k < 2 * near
        far = jnp.where(both, k // 2 + 1, k - near + 1)
        left = jnp.where(both, k % 2, jnp.where(z > owners - 1 - z, 0, 1)) == 0
        return jnp.where(left, z - far, z + far), left

    def arrive(k, kv):
        owner, left = source(k)
        block = corpus_ref.at[owner, mine, kv]
        side = side_copy(block, owner, kv)
        line_copy(block, owner, kv, 1).wait_recv()

        @pl.when(jnp.logical_and(left, has_right))
        def _():
            line_copy(block, owner, kv, 1).start()

        @pl.when(jnp.logical_and(jnp.logical_not(left), has_left))
        def _():
            line_copy(block, owner, kv, 0).start()

        side.start()

    def compute(owner, kv):
        side_copy(corpus_ref.at[owner, mine, kv], owner, kv).wait_recv()
        if kv == 0:
            for h in range(2):
                edge = edge_ref[:, h * half_len:(h + 1) * half_len]
                for s in range(slots):
                    at = slice((h * slots + s) * half_len, (h * slots + s + 1) * half_len)
                    held = jnp.where(entry_ref[...] == owner * slots + s,
                                     live_ref[:, h * half_len:(h + 1) * half_len], 0.0)
                    count = jnp.dot(before_ref[...], held.astype(jnp.bfloat16),
                                    preferred_element_type=jnp.float32)
                    total = count + jnp.where(
                        slot_ref[...] == owner * slots + s, edge, 0.0)
                    bias_ref[:, at] = jnp.where(
                        total > 0.5, jnp.log2(jnp.maximum(total, 1.0)), MASKED)
        for h in range(2):
            value_ref[h * half:(h + 1) * half, :head_dim] = corpus_ref[owner, h, kv, 1]
        keys = lambda: corpus_ref[owner, :, kv, 0].reshape(2 * half, head_dim)
        attend(q_ref, kv, (keys, kv_local), value_ref, bias_ref, acc_ref, max_ref, False,
               score_scale, pair)

    corpus_ref[z, mine] = own_ref[...]
    new_ref[mine] = fresh_ref[...]
    value_ref[:, head_dim:] = jnp.ones((2 * half, head_dim), jnp.bfloat16)
    new_value_ref[:, head_dim:] = jnp.ones((2 * new_half, head_dim), jnp.bfloat16)
    npass, recomputed, stored = chosen_ref.shape[1], again_ref.shape[1], place_ref.shape[1]
    iota = lambda shape, dim: lax.broadcasted_iota(jnp.int32, shape, dim)

    def column(row, length, start):
        shape = (length, row.shape[1])
        return jnp.sum(jnp.where(iota(shape, 1) == iota(shape, 0) + start, row, 0),
                       axis=1, keepdims=True)

    chosen, again = chosen_ref[...], again_ref[...]
    shape = (npass, stored)
    entry = jnp.sum(jnp.where(column(chosen, npass, 0) == iota(shape, 1), place_ref[...], 0),
                    axis=1, keepdims=True)
    entry_ref[...] = entry
    shape = (npass, npass)
    entry_row = jnp.sum(jnp.where(iota(shape, 0) == iota(shape, 1), entry, 0), axis=0,
                        keepdims=True)
    in_passage = again // plen == iota((npass, recomputed), 0)
    at_token = column(again, recomputed, 0) % plen == iota((recomputed, plen), 1)
    replaced = jnp.dot(jnp.where(in_passage, 1.0, 0.0).astype(jnp.bfloat16),
                       jnp.where(at_token, 1.0, 0.0).astype(jnp.bfloat16),
                       preferred_element_type=jnp.float32)
    live = jnp.where(replaced > 0.5, 0.0, 1.0)
    live_ref[...] = live
    index = iota((rows, 1), 0) + mine * rows
    row_pos = jnp.where(index < recomputed, column(again, rows, mine * rows),
                        npass * plen + index - recomputed)
    row_pass = row_pos // plen
    shape = (rows, npass)
    within = row_pass == iota(shape, 1)
    before_ref[...] = jnp.where(iota(shape, 1) < row_pass, 1.0, 0.0).astype(jnp.bfloat16)
    slot_ref[...] = jnp.sum(jnp.where(within, entry_row + 1, 0), axis=1, keepdims=True) - 1
    edge_ref[...] = jnp.where(
        iota((rows, plen), 1) <= row_pos % plen,
        jnp.dot(jnp.where(within, 1.0, 0.0).astype(jnp.bfloat16), live.astype(jnp.bfloat16),
                preferred_element_type=jnp.float32), 0.0)
    row = lax.broadcasted_iota(jnp.int32, (rows, 2 * new_half), 0) + mine * rows
    column = lax.broadcasted_iota(jnp.int32, (rows, 2 * new_half), 1)
    new_bias_ref[...] = jnp.where(column <= row, 0.0, MASKED)

    new_copy.wait_recv()
    for kv in range(kv_local):
        for h in range(2):
            new_value_ref[h * new_half:(h + 1) * new_half, :head_dim] = new_ref[h, kv, 1]
        keys = lambda: new_ref[:, kv, 0].reshape(2 * new_half, head_dim)
        attend(q_ref, kv, (keys, kv_local), new_value_ref, new_bias_ref, acc_ref, max_ref, True,
               score_scale, pair)

    for kv in range(kv_local - 1):
        compute(z, kv)

    def turn(k, carry):
        for kv in range(kv_local):
            arrive(k, kv)
            if kv == 0:
                compute(jnp.where(k == 0, z, source(jnp.maximum(k - 1, 0))[0]), kv_local - 1)
            else:
                compute(source(k)[0], kv - 1)
        return carry

    lax.fori_loop(0, owners - 1, turn, 0)
    compute(source(owners - 2)[0], kv_local - 1)

    for head in range(heads):
        total = acc_ref[head]
        out_ref[:, head * head_dim:(head + 1) * head_dim] = (
            total[:, :head_dim] / total[:, head_dim:]
        ).astype(out_ref.dtype)

    for kv in range(kv_local):
        @pl.when(has_left)
        def _():
            line_copy(own_ref.at[kv], z, kv, 0).wait_send()

        @pl.when(has_right)
        def _():
            line_copy(own_ref.at[kv], z, kv, 1).wait_send()

        side_copy(own_ref.at[kv], z, kv).wait_send()
    new_copy.wait_send()

    def sent(k, carry):
        owner, left = source(k)
        for kv in range(kv_local):
            block = corpus_ref.at[owner, mine, kv]

            @pl.when(jnp.logical_and(left, has_right))
            def _():
                line_copy(block, owner, kv, 1).wait_send()

            @pl.when(jnp.logical_and(jnp.logical_not(left), has_left))
            def _():
                line_copy(block, owner, kv, 0).wait_send()

            side_copy(block, owner, kv).wait_send()
        return carry

    lax.fori_loop(0, owners - 1, sent, 0)


def on_device(cache_kv, passage_slot, retrieval, recompute, new_q, new_kv):
    slots, half_len, kv_local, _, head_dim = cache_kv.shape
    npass = retrieval.shape[1]
    new_rows, heads = new_q.shape[1:3]
    owners = lax.axis_size("cache")
    holders = lax.axis_size("kvsplit")
    half_index = lax.axis_index("kvsplit")
    plen = half_len * holders
    rows = new_rows // holders

    own = cache_kv.transpose(2, 3, 0, 1, 4).reshape(kv_local, 2, slots * half_len, head_dim)
    fresh = new_kv[0].transpose(1, 2, 0, 3)

    keys = holders * slots * half_len
    queries = lax.dynamic_slice_in_dim(new_q[0], half_index * rows, rows, 0).transpose(1, 0, 2)
    score_scale = head_dim ** (-0.5) * math.log2(math.e)
    dma = pltpu.SemaphoreType.DMA
    result = pl.pallas_call(
        functools.partial(kernel, score_scale, 1, owners),
        out_shape=jax.ShapeDtypeStruct((rows, heads * head_dim), jnp.bfloat16),
        in_specs=[pl.BlockSpec(memory_space=pltpu.VMEM)] * 6,
        out_specs=pl.BlockSpec(memory_space=pltpu.VMEM),
        scratch_shapes=[
            pltpu.VMEM((heads, rows, 2 * head_dim), jnp.float32),
            pltpu.VMEM((heads, rows, head_dim), jnp.float32),
            pltpu.VMEM((keys, 2 * head_dim), jnp.bfloat16),
            pltpu.VMEM((new_rows, 2 * head_dim), jnp.bfloat16),
            pltpu.VMEM((rows, keys), jnp.float32),
            pltpu.VMEM((rows, new_rows), jnp.float32),
            pltpu.VMEM((rows, plen), jnp.float32),
            pltpu.VMEM((npass, plen), jnp.float32),
            pltpu.VMEM((rows, npass), jnp.bfloat16),
            pltpu.VMEM((rows, 1), jnp.int32),
            pltpu.VMEM((npass, 1), jnp.int32),
            pltpu.VMEM((owners, holders) + own.shape, jnp.bfloat16),
            pltpu.VMEM((holders,) + fresh.shape, jnp.bfloat16),
            dma((2, owners, kv_local)),
            dma((owners, kv_local)),
            dma((owners, kv_local)),
            dma((owners, kv_local)),
            dma(()),
            dma(()),
        ],
        compiler_params=pltpu.CompilerParams(
            vmem_limit_bytes=56 * 1024 * 1024, collective_id=0, has_side_effects=True),
    )(queries, fresh, own, passage_slot[None, :], retrieval, recompute)
    return result[None]


def solution(mesh):
    in_specs = (
        P(("group", "cache"), "kvsplit", "tensor", None, None),
        P("group"),
        P(("group", "cache"), None),
        P(("group", "cache"), None),
        P(("group", "cache"), None, "tensor", None),
        P(("group", "cache"), "kvsplit", "tensor", None, None),
    )
    out_specs = P(("group", "cache"), "kvsplit", "tensor")
    return jax.shard_map(
        on_device, mesh=mesh, in_specs=in_specs, out_specs=out_specs, check_vma=False
    )
```

```python
import functools
import math

import jax
import jax.numpy as jnp
from jax import lax
from jax.experimental import pallas as pl
from jax.experimental.pallas import tpu as pltpu
from jax.sharding import PartitionSpec as P

MASKED = -1e30


MESH = pl.DeviceIdType.MESH


def attend(q_ref, kv, keys, value_ref, bias_ref, acc_ref, max_ref, first, score_scale, pair):
    heads, rows, head_dim = q_ref.shape
    group = heads // keys[1]
    pairs = group // pair

    for i in range(pairs):
        at = slice(kv * group + i * pair, kv * group + (i + 1) * pair)
        query = q_ref[at].reshape(pair * rows, head_dim)
        scores = lax.dot_general(
            query, keys[0](), (((1,), (1,)), ((), ())), preferred_element_type=jnp.float32
        )
        scores = scores.reshape(pair, rows, -1) * score_scale + bias_ref[...][None]
        block_max = jnp.max(scores, axis=2, keepdims=True)
        if first:
            row_max = jnp.broadcast_to(block_max, (pair, rows, head_dim))
        else:
            former = max_ref[at]
            row_max = jnp.maximum(former, block_max)
        weights = jnp.exp2(scores - row_max[:, :, :1]).astype(jnp.bfloat16)
        part = jnp.dot(
            weights.reshape(pair * rows, -1), value_ref[...], preferred_element_type=jnp.float32
        ).reshape(pair, rows, 2 * head_dim)
        if first:
            acc_ref[at] = part
        else:
            shrink = jnp.exp2(former - row_max)
            acc_ref[at] = acc_ref[at] * jnp.concatenate([shrink, shrink], axis=2) + part
        max_ref[at] = row_max


def kernel(score_scale, pair, owners, q_ref, fresh_ref, own_ref, place_ref, chosen_ref, again_ref,
           out_ref,
           acc_ref, max_ref, value_ref, new_value_ref, bias_ref, new_bias_ref, edge_ref,
           live_ref, before_ref, slot_ref, entry_ref, corpus_ref, new_ref, line_send, line_recv, side_send, side_recv, new_send, new_recv):
    heads, rows, head_dim = q_ref.shape
    kv_local, _, half, _ = own_ref.shape
    new_half = fresh_ref.shape[2]
    plen = live_ref.shape[1]
    half_len = plen // 2
    slots = half // half_len
    z = lax.axis_index("cache")
    mine = lax.axis_index("kvsplit")
    other = 1 - mine
    has_left, has_right = z > 0, z < owners - 1

    barrier = pltpu.get_barrier_semaphore()
    pl.semaphore_signal(barrier, inc=1, device_id={"kvsplit": other}, device_id_type=MESH)

    @pl.when(has_left)
    def _():
        pl.semaphore_signal(barrier, inc=1, device_id={"cache": z - 1}, device_id_type=MESH)

    @pl.when(has_right)
    def _():
        pl.semaphore_signal(barrier, inc=1, device_id={"cache": z + 1}, device_id_type=MESH)

    peers = 1 + jnp.minimum(z, 1) + jnp.minimum(owners - 1 - z, 1)
    pl.semaphore_wait(barrier, peers)

    def line_copy(block, owner, kv, way):
        return pltpu.make_async_remote_copy(
            src_ref=block, dst_ref=corpus_ref.at[owner, mine, kv],
            send_sem=line_send.at[way, owner, kv], recv_sem=line_recv.at[owner, kv],
            device_id={"cache": z + 1 if way else z - 1}, device_id_type=MESH)

    def side_copy(block, owner, kv):
        return pltpu.make_async_remote_copy(
            src_ref=block, dst_ref=corpus_ref.at[owner, mine, kv],
            send_sem=side_send.at[owner, kv], recv_sem=side_recv.at[owner, kv],
            device_id={"kvsplit": other}, device_id_type=MESH)

    new_copy = pltpu.make_async_remote_copy(
        src_ref=fresh_ref, dst_ref=new_ref.at[mine], send_sem=new_send, recv_sem=new_recv,
        device_id={"kvsplit": other}, device_id_type=MESH)

    for kv in range(kv_local):
        @pl.when(has_left)
        def _():
            line_copy(own_ref.at[kv], z, kv, 0).start()

        @pl.when(has_right)
        def _():
            line_copy(own_ref.at[kv], z, kv, 1).start()

    new_copy.start()
    for kv in range(kv_local):
        side_copy(own_ref.at[kv], z, kv).start()

    near = jnp.minimum(z, owners - 1 - z)

    def source(k):
        both = k < 2 * near
        far = jnp.where(both, k // 2 + 1, k - near + 1)
        left = jnp.where(both, k % 2, jnp.where(z > owners - 1 - z, 0, 1)) == 0
        return jnp.where(left, z - far, z + far), left

    def arrive(unit):
        both = unit < 2 * near * kv_local
        turn = unit % (2 * kv_local)
        k = jnp.where(both, unit // (2 * kv_local) * 2 + turn % 2, unit // kv_local)
        kv = jnp.where(both, turn // 2, unit % kv_local)
        owner, left = source(k)
        block = corpus_ref.at[owner, mine, kv]
        side = side_copy(block, owner, kv)
        line_copy(block, owner, kv, 1).wait_recv()

        @pl.when(jnp.logical_and(left, has_right))
        def _():
            line_copy(block, owner, kv, 1).start()

        @pl.when(jnp.logical_and(jnp.logical_not(left), has_left))
        def _():
            line_copy(block, owner, kv, 0).start()

        side.start()

    def compute(owner, kv):
        side_copy(corpus_ref.at[owner, mine, kv], owner, kv).wait_recv()
        if kv == 0:
            for h in range(2):
                edge = edge_ref[:, h * half_len:(h + 1) * half_len]
                for s in range(slots):
                    at = slice((h * slots + s) * half_len, (h * slots + s + 1) * half_len)
                    held = jnp.where(entry_ref[...] == owner * slots + s,
                                     live_ref[:, h * half_len:(h + 1) * half_len], 0.0)
                    count = jnp.dot(before_ref[...], held.astype(jnp.bfloat16),
                                    preferred_element_type=jnp.float32)
                    total = count + jnp.where(
                        slot_ref[...] == owner * slots + s, edge, 0.0)
                    bias_ref[:, at] = jnp.where(
                        total > 0.5, jnp.log2(jnp.maximum(total, 1.0)), MASKED)
        for h in range(2):
            value_ref[h * half:(h + 1) * half, :head_dim] = corpus_ref[owner, h, kv, 1]
        keys = lambda: corpus_ref[owner, :, kv, 0].reshape(2 * half, head_dim)
        attend(q_ref, kv, (keys, kv_local), value_ref, bias_ref, acc_ref, max_ref, False,
               score_scale, pair)

    corpus_ref[z, mine] = own_ref[...]
    new_ref[mine] = fresh_ref[...]
    value_ref[:, head_dim:] = jnp.ones((2 * half, head_dim), jnp.bfloat16)
    new_value_ref[:, head_dim:] = jnp.ones((2 * new_half, head_dim), jnp.bfloat16)
    npass, recomputed, stored = chosen_ref.shape[1], again_ref.shape[1], place_ref.shape[1]
    iota = lambda shape, dim: lax.broadcasted_iota(jnp.int32, shape, dim)

    def column(row, length, start):
        shape = (length, row.shape[1])
        return jnp.sum(jnp.where(iota(shape, 1) == iota(shape, 0) + start, row, 0),
                       axis=1, keepdims=True)

    chosen, again = chosen_ref[...], again_ref[...]
    shape = (npass, stored)
    entry = jnp.sum(jnp.where(column(chosen, npass, 0) == iota(shape, 1), place_ref[...], 0),
                    axis=1, keepdims=True)
    entry_ref[...] = entry
    shape = (npass, npass)
    entry_row = jnp.sum(jnp.where(iota(shape, 0) == iota(shape, 1), entry, 0), axis=0,
                        keepdims=True)
    in_passage = again // plen == iota((npass, recomputed), 0)
    at_token = column(again, recomputed, 0) % plen == iota((recomputed, plen), 1)
    replaced = jnp.dot(jnp.where(in_passage, 1.0, 0.0).astype(jnp.bfloat16),
                       jnp.where(at_token, 1.0, 0.0).astype(jnp.bfloat16),
                       preferred_element_type=jnp.float32)
    live = jnp.where(replaced > 0.5, 0.0, 1.0)
    live_ref[...] = live
    index = iota((rows, 1), 0) + mine * rows
    row_pos = jnp.where(index < recomputed, column(again, rows, mine * rows),
                        npass * plen + index - recomputed)
    row_pass = row_pos // plen
    shape = (rows, npass)
    within = row_pass == iota(shape, 1)
    before_ref[...] = jnp.where(iota(shape, 1) < row_pass, 1.0, 0.0).astype(jnp.bfloat16)
    slot_ref[...] = jnp.sum(jnp.where(within, entry_row + 1, 0), axis=1, keepdims=True) - 1
    edge_ref[...] = jnp.where(
        iota((rows, plen), 1) <= row_pos % plen,
        jnp.dot(jnp.where(within, 1.0, 0.0).astype(jnp.bfloat16), live.astype(jnp.bfloat16),
                preferred_element_type=jnp.float32), 0.0)
    row = lax.broadcasted_iota(jnp.int32, (rows, 2 * new_half), 0) + mine * rows
    column = lax.broadcasted_iota(jnp.int32, (rows, 2 * new_half), 1)
    new_bias_ref[...] = jnp.where(column <= row, 0.0, MASKED)

    new_copy.wait_recv()
    for kv in range(kv_local):
        for h in range(2):
            new_value_ref[h * new_half:(h + 1) * new_half, :head_dim] = new_ref[h, kv, 1]
        keys = lambda: new_ref[:, kv, 0].reshape(2 * new_half, head_dim)
        attend(q_ref, kv, (keys, kv_local), new_value_ref, new_bias_ref, acc_ref, max_ref, True,
               score_scale, pair)

    for kv in range(kv_local - 1):
        compute(z, kv)

    def turn(k, carry):
        for kv in range(kv_local):
            arrive(k * kv_local + kv)
            if kv == 0:
                compute(jnp.where(k == 0, z, source(jnp.maximum(k - 1, 0))[0]), kv_local - 1)
            else:
                compute(source(k)[0], kv - 1)
        return carry

    lax.fori_loop(0, owners - 1, turn, 0)
    compute(source(owners - 2)[0], kv_local - 1)

    for head in range(heads):
        total = acc_ref[head]
        out_ref[:, head * head_dim:(head + 1) * head_dim] = (
            total[:, :head_dim] / total[:, head_dim:]
        ).astype(out_ref.dtype)

    for kv in range(kv_local):
        @pl.when(has_left)
        def _():
            line_copy(own_ref.at[kv], z, kv, 0).wait_send()

        @pl.when(has_right)
        def _():
            line_copy(own_ref.at[kv], z, kv, 1).wait_send()

        side_copy(own_ref.at[kv], z, kv).wait_send()
    new_copy.wait_send()

    def sent(k, carry):
        owner, left = source(k)
        for kv in range(kv_local):
            block = corpus_ref.at[owner, mine, kv]

            @pl.when(jnp.logical_and(left, has_right))
            def _():
                line_copy(block, owner, kv, 1).wait_send()

            @pl.when(jnp.logical_and(jnp.logical_not(left), has_left))
            def _():
                line_copy(block, owner, kv, 0).wait_send()

            side_copy(block, owner, kv).wait_send()
        return carry

    lax.fori_loop(0, owners - 1, sent, 0)


def on_device(cache_kv, passage_slot, retrieval, recompute, new_q, new_kv):
    slots, half_len, kv_local, _, head_dim = cache_kv.shape
    npass = retrieval.shape[1]
    new_rows, heads = new_q.shape[1:3]
    owners = lax.axis_size("cache")
    holders = lax.axis_size("kvsplit")
    half_index = lax.axis_index("kvsplit")
    plen = half_len * holders
    rows = new_rows // holders

    own = cache_kv.transpose(2, 3, 0, 1, 4).reshape(kv_local, 2, slots * half_len, head_dim)
    fresh = new_kv[0].transpose(1, 2, 0, 3)

    keys = holders * slots * half_len
    queries = lax.dynamic_slice_in_dim(new_q[0], half_index * rows, rows, 0).transpose(1, 0, 2)
    score_scale = head_dim ** (-0.5) * math.log2(math.e)
    dma = pltpu.SemaphoreType.DMA
    result = pl.pallas_call(
        functools.partial(kernel, score_scale, 1, owners),
        out_shape=jax.ShapeDtypeStruct((rows, heads * head_dim), jnp.bfloat16),
        in_specs=[pl.BlockSpec(memory_space=pltpu.VMEM)] * 6,
        out_specs=pl.BlockSpec(memory_space=pltpu.VMEM),
        scratch_shapes=[
            pltpu.VMEM((heads, rows, 2 * head_dim), jnp.float32),
            pltpu.VMEM((heads, rows, head_dim), jnp.float32),
            pltpu.VMEM((keys, 2 * head_dim), jnp.bfloat16),
            pltpu.VMEM((new_rows, 2 * head_dim), jnp.bfloat16),
            pltpu.VMEM((rows, keys), jnp.float32),
            pltpu.VMEM((rows, new_rows), jnp.float32),
            pltpu.VMEM((rows, plen), jnp.float32),
            pltpu.VMEM((npass, plen), jnp.float32),
            pltpu.VMEM((rows, npass), jnp.bfloat16),
            pltpu.VMEM((rows, 1), jnp.int32),
            pltpu.VMEM((npass, 1), jnp.int32),
            pltpu.VMEM((owners, holders) + own.shape, jnp.bfloat16),
            pltpu.VMEM((holders,) + fresh.shape, jnp.bfloat16),
            dma((2, owners, kv_local)),
            dma((owners, kv_local)),
            dma((owners, kv_local)),
            dma((owners, kv_local)),
            dma(()),
            dma(()),
        ],
        compiler_params=pltpu.CompilerParams(
            vmem_limit_bytes=56 * 1024 * 1024, collective_id=0, has_side_effects=True),
    )(queries, fresh, own, passage_slot[None, :], retrieval, recompute)
    return result[None]


def solution(mesh):
    in_specs = (
        P(("group", "cache"), "kvsplit", "tensor", None, None),
        P("group"),
        P(("group", "cache"), None),
        P(("group", "cache"), None),
        P(("group", "cache"), None, "tensor", None),
        P(("group", "cache"), "kvsplit", "tensor", None, None),
    )
    out_specs = P(("group", "cache"), "kvsplit", "tensor")
    return jax.shard_map(
        on_device, mesh=mesh, in_specs=in_specs, out_specs=out_specs, check_vma=False
    )
```

```python
import functools
import math

import jax
import jax.numpy as jnp
from jax import lax
from jax.experimental import pallas as pl
from jax.experimental.pallas import tpu as pltpu
from jax.sharding import PartitionSpec as P

MASKED = -1e30


MESH = pl.DeviceIdType.MESH


def attend(q_ref, kv, keys, value_ref, bias_ref, acc_ref, max_ref, first, score_scale, pair):
    heads, rows, head_dim = q_ref.shape
    group = heads // keys[1]
    pairs = group // pair

    for i in range(pairs):
        at = slice(kv * group + i * pair, kv * group + (i + 1) * pair)
        query = q_ref[at].reshape(pair * rows, head_dim)
        scores = lax.dot_general(
            query, keys[0](), (((1,), (1,)), ((), ())), preferred_element_type=jnp.float32
        )
        scores = scores.reshape(pair, rows, -1) * score_scale + bias_ref[...][None]
        block_max = jnp.max(scores, axis=2, keepdims=True)
        if first:
            row_max = jnp.broadcast_to(block_max, (pair, rows, head_dim))
        else:
            former = max_ref[at]
            row_max = jnp.maximum(former, block_max)
        weights = jnp.exp2(scores - row_max[:, :, :1]).astype(jnp.bfloat16)
        part = jnp.dot(
            weights.reshape(pair * rows, -1), value_ref[...], preferred_element_type=jnp.float32
        ).reshape(pair, rows, 2 * head_dim)
        if first:
            acc_ref[at] = part
        else:
            shrink = jnp.exp2(former - row_max)
            acc_ref[at] = acc_ref[at] * jnp.concatenate([shrink, shrink], axis=2) + part
        max_ref[at] = row_max


def kernel(score_scale, pair, owners, q_ref, fresh_ref, own_ref, place_ref, chosen_ref, again_ref,
           out_ref,
           acc_ref, max_ref, value_ref, new_value_ref, bias_ref, new_bias_ref, edge_ref,
           live_ref, before_ref, slot_ref, entry_ref, corpus_ref, new_ref, line_send, line_recv, side_send, side_recv, new_send, new_recv):
    heads, rows, head_dim = q_ref.shape
    kv_local, _, half, _ = own_ref.shape
    new_half = fresh_ref.shape[2]
    plen = live_ref.shape[1]
    half_len = plen // 2
    slots = half // half_len
    z = lax.axis_index("cache")
    mine = lax.axis_index("kvsplit")
    other = 1 - mine
    has_left, has_right = z > 0, z < owners - 1

    barrier = pltpu.get_barrier_semaphore()
    pl.semaphore_signal(barrier, inc=1, device_id={"kvsplit": other}, device_id_type=MESH)

    @pl.when(has_left)
    def _():
        pl.semaphore_signal(barrier, inc=1, device_id={"cache": z - 1}, device_id_type=MESH)

    @pl.when(has_right)
    def _():
        pl.semaphore_signal(barrier, inc=1, device_id={"cache": z + 1}, device_id_type=MESH)

    peers = 1 + jnp.minimum(z, 1) + jnp.minimum(owners - 1 - z, 1)
    pl.semaphore_wait(barrier, peers)

    def line_copy(block, owner, kv, way, piece):
        return pltpu.make_async_remote_copy(
            src_ref=block.at[piece], dst_ref=corpus_ref.at[owner, mine, kv, piece],
            send_sem=line_send.at[way, owner, kv, piece],
            recv_sem=line_recv.at[owner, kv, piece],
            device_id={"cache": z + 1 if way else z - 1}, device_id_type=MESH)

    def side_copy(block, owner, kv):
        return pltpu.make_async_remote_copy(
            src_ref=block, dst_ref=corpus_ref.at[owner, mine, kv],
            send_sem=side_send.at[owner, kv], recv_sem=side_recv.at[owner, kv],
            device_id={"kvsplit": other}, device_id_type=MESH)

    new_copy = pltpu.make_async_remote_copy(
        src_ref=fresh_ref, dst_ref=new_ref.at[mine], send_sem=new_send, recv_sem=new_recv,
        device_id={"kvsplit": other}, device_id_type=MESH)

    for kv in range(kv_local):
        @pl.when(has_left)
        def _():
            for piece in range(2):
                line_copy(own_ref.at[kv], z, kv, 0, piece).start()

        @pl.when(has_right)
        def _():
            for piece in range(2):
                line_copy(own_ref.at[kv], z, kv, 1, piece).start()

    new_copy.start()
    for kv in range(kv_local):
        side_copy(own_ref.at[kv], z, kv).start()

    near = jnp.minimum(z, owners - 1 - z)

    def source(k):
        both = k < 2 * near
        far = jnp.where(both, k // 2 + 1, k - near + 1)
        left = jnp.where(both, k % 2, jnp.where(z > owners - 1 - z, 0, 1)) == 0
        return jnp.where(left, z - far, z + far), left

    def arrive(unit):
        both = unit < 2 * near * kv_local
        turn = unit % (2 * kv_local)
        k = jnp.where(both, unit // (2 * kv_local) * 2 + turn % 2, unit // kv_local)
        kv = jnp.where(both, turn // 2, unit % kv_local)
        owner, left = source(k)
        block = corpus_ref.at[owner, mine, kv]
        side = side_copy(block, owner, kv)
        for piece in range(2):
            line_copy(block, owner, kv, 1, piece).wait_recv()

            @pl.when(jnp.logical_and(left, has_right))
            def _():
                line_copy(block, owner, kv, 1, piece).start()

            @pl.when(jnp.logical_and(jnp.logical_not(left), has_left))
            def _():
                line_copy(block, owner, kv, 0, piece).start()

        side.start()

    def compute(owner, kv):
        side_copy(corpus_ref.at[owner, mine, kv], owner, kv).wait_recv()
        if kv == 0:
            for h in range(2):
                edge = edge_ref[:, h * half_len:(h + 1) * half_len]
                for s in range(slots):
                    at = slice((h * slots + s) * half_len, (h * slots + s + 1) * half_len)
                    held = jnp.where(entry_ref[...] == owner * slots + s,
                                     live_ref[:, h * half_len:(h + 1) * half_len], 0.0)
                    count = jnp.dot(before_ref[...], held.astype(jnp.bfloat16),
                                    preferred_element_type=jnp.float32)
                    total = count + jnp.where(
                        slot_ref[...] == owner * slots + s, edge, 0.0)
                    bias_ref[:, at] = jnp.where(
                        total > 0.5, jnp.log2(jnp.maximum(total, 1.0)), MASKED)
        for h in range(2):
            value_ref[h * half:(h + 1) * half, :head_dim] = corpus_ref[owner, h, kv, 1]
        keys = lambda: corpus_ref[owner, :, kv, 0].reshape(2 * half, head_dim)
        attend(q_ref, kv, (keys, kv_local), value_ref, bias_ref, acc_ref, max_ref, False,
               score_scale, pair)

    corpus_ref[z, mine] = own_ref[...]
    new_ref[mine] = fresh_ref[...]
    value_ref[:, head_dim:] = jnp.ones((2 * half, head_dim), jnp.bfloat16)
    new_value_ref[:, head_dim:] = jnp.ones((2 * new_half, head_dim), jnp.bfloat16)
    npass, recomputed, stored = chosen_ref.shape[1], again_ref.shape[1], place_ref.shape[1]
    iota = lambda shape, dim: lax.broadcasted_iota(jnp.int32, shape, dim)

    def column(row, length, start):
        shape = (length, row.shape[1])
        return jnp.sum(jnp.where(iota(shape, 1) == iota(shape, 0) + start, row, 0),
                       axis=1, keepdims=True)

    chosen, again = chosen_ref[...], again_ref[...]
    shape = (npass, stored)
    entry = jnp.sum(jnp.where(column(chosen, npass, 0) == iota(shape, 1), place_ref[...], 0),
                    axis=1, keepdims=True)
    entry_ref[...] = entry
    shape = (npass, npass)
    entry_row = jnp.sum(jnp.where(iota(shape, 0) == iota(shape, 1), entry, 0), axis=0,
                        keepdims=True)
    in_passage = again // plen == iota((npass, recomputed), 0)
    at_token = column(again, recomputed, 0) % plen == iota((recomputed, plen), 1)
    replaced = jnp.dot(jnp.where(in_passage, 1.0, 0.0).astype(jnp.bfloat16),
                       jnp.where(at_token, 1.0, 0.0).astype(jnp.bfloat16),
                       preferred_element_type=jnp.float32)
    live = jnp.where(replaced > 0.5, 0.0, 1.0)
    live_ref[...] = live
    index = iota((rows, 1), 0) + mine * rows
    row_pos = jnp.where(index < recomputed, column(again, rows, mine * rows),
                        npass * plen + index - recomputed)
    row_pass = row_pos // plen
    shape = (rows, npass)
    within = row_pass == iota(shape, 1)
    before_ref[...] = jnp.where(iota(shape, 1) < row_pass, 1.0, 0.0).astype(jnp.bfloat16)
    slot_ref[...] = jnp.sum(jnp.where(within, entry_row + 1, 0), axis=1, keepdims=True) - 1
    edge_ref[...] = jnp.where(
        iota((rows, plen), 1) <= row_pos % plen,
        jnp.dot(jnp.where(within, 1.0, 0.0).astype(jnp.bfloat16), live.astype(jnp.bfloat16),
                preferred_element_type=jnp.float32), 0.0)
    row = lax.broadcasted_iota(jnp.int32, (rows, 2 * new_half), 0) + mine * rows
    column = lax.broadcasted_iota(jnp.int32, (rows, 2 * new_half), 1)
    new_bias_ref[...] = jnp.where(column <= row, 0.0, MASKED)

    new_copy.wait_recv()
    for kv in range(kv_local):
        for h in range(2):
            new_value_ref[h * new_half:(h + 1) * new_half, :head_dim] = new_ref[h, kv, 1]
        keys = lambda: new_ref[:, kv, 0].reshape(2 * new_half, head_dim)
        attend(q_ref, kv, (keys, kv_local), new_value_ref, new_bias_ref, acc_ref, max_ref, True,
               score_scale, pair)

    for kv in range(kv_local - 1):
        compute(z, kv)

    def turn(k, carry):
        for kv in range(kv_local):
            arrive(k * kv_local + kv)
            if kv == 0:
                compute(jnp.where(k == 0, z, source(jnp.maximum(k - 1, 0))[0]), kv_local - 1)
            else:
                compute(source(k)[0], kv - 1)
        return carry

    lax.fori_loop(0, owners - 1, turn, 0)
    compute(source(owners - 2)[0], kv_local - 1)

    for head in range(heads):
        total = acc_ref[head]
        out_ref[:, head * head_dim:(head + 1) * head_dim] = (
            total[:, :head_dim] / total[:, head_dim:]
        ).astype(out_ref.dtype)

    for kv in range(kv_local):
        @pl.when(has_left)
        def _():
            for piece in range(2):
                line_copy(own_ref.at[kv], z, kv, 0, piece).wait_send()

        @pl.when(has_right)
        def _():
            for piece in range(2):
                line_copy(own_ref.at[kv], z, kv, 1, piece).wait_send()

        side_copy(own_ref.at[kv], z, kv).wait_send()
    new_copy.wait_send()

    def sent(k, carry):
        owner, left = source(k)
        for kv in range(kv_local):
            block = corpus_ref.at[owner, mine, kv]

            @pl.when(jnp.logical_and(left, has_right))
            def _():
                for piece in range(2):
                    line_copy(block, owner, kv, 1, piece).wait_send()

            @pl.when(jnp.logical_and(jnp.logical_not(left), has_left))
            def _():
                for piece in range(2):
                    line_copy(block, owner, kv, 0, piece).wait_send()

            side_copy(block, owner, kv).wait_send()
        return carry

    lax.fori_loop(0, owners - 1, sent, 0)


def on_device(cache_kv, passage_slot, retrieval, recompute, new_q, new_kv):
    slots, half_len, kv_local, _, head_dim = cache_kv.shape
    npass = retrieval.shape[1]
    new_rows, heads = new_q.shape[1:3]
    owners = lax.axis_size("cache")
    holders = lax.axis_size("kvsplit")
    half_index = lax.axis_index("kvsplit")
    plen = half_len * holders
    rows = new_rows // holders

    own = cache_kv.transpose(2, 3, 0, 1, 4).reshape(kv_local, 2, slots * half_len, head_dim)
    fresh = new_kv[0].transpose(1, 2, 0, 3)

    keys = holders * slots * half_len
    queries = lax.dynamic_slice_in_dim(new_q[0], half_index * rows, rows, 0).transpose(1, 0, 2)
    score_scale = head_dim ** (-0.5) * math.log2(math.e)
    dma = pltpu.SemaphoreType.DMA
    result = pl.pallas_call(
        functools.partial(kernel, score_scale, 1, owners),
        out_shape=jax.ShapeDtypeStruct((rows, heads * head_dim), jnp.bfloat16),
        in_specs=[pl.BlockSpec(memory_space=pltpu.VMEM)] * 6,
        out_specs=pl.BlockSpec(memory_space=pltpu.VMEM),
        scratch_shapes=[
            pltpu.VMEM((heads, rows, 2 * head_dim), jnp.float32),
            pltpu.VMEM((heads, rows, head_dim), jnp.float32),
            pltpu.VMEM((keys, 2 * head_dim), jnp.bfloat16),
            pltpu.VMEM((new_rows, 2 * head_dim), jnp.bfloat16),
            pltpu.VMEM((rows, keys), jnp.float32),
            pltpu.VMEM((rows, new_rows), jnp.float32),
            pltpu.VMEM((rows, plen), jnp.float32),
            pltpu.VMEM((npass, plen), jnp.float32),
            pltpu.VMEM((rows, npass), jnp.bfloat16),
            pltpu.VMEM((rows, 1), jnp.int32),
            pltpu.VMEM((npass, 1), jnp.int32),
            pltpu.VMEM((owners, holders) + own.shape, jnp.bfloat16),
            pltpu.VMEM((holders,) + fresh.shape, jnp.bfloat16),
            dma((2, owners, kv_local, 2)),
            dma((owners, kv_local, 2)),
            dma((owners, kv_local)),
            dma((owners, kv_local)),
            dma(()),
            dma(()),
        ],
        compiler_params=pltpu.CompilerParams(
            vmem_limit_bytes=56 * 1024 * 1024, collective_id=0, has_side_effects=True),
    )(queries, fresh, own, passage_slot[None, :], retrieval, recompute)
    return result[None]


def solution(mesh):
    in_specs = (
        P(("group", "cache"), "kvsplit", "tensor", None, None),
        P("group"),
        P(("group", "cache"), None),
        P(("group", "cache"), None),
        P(("group", "cache"), None, "tensor", None),
        P(("group", "cache"), "kvsplit", "tensor", None, None),
    )
    out_specs = P(("group", "cache"), "kvsplit", "tensor")
    return jax.shard_map(
        on_device, mesh=mesh, in_specs=in_specs, out_specs=out_specs, check_vma=False
    )
```
